32 devices in a mesh: section: 8 (over y, x, core), dp: 4 (over z).
Axes of the slice: x: 2, y: 2, z: 4, core: 2. Of those that a mesh axis runs over, the one named last changes fastest.
Arguments:
- images: bfloat16 [12, 256, 512], P(None, 'dp'), may hold values from -6 to 6
- cotangent: bfloat16 [12, 256, 512], P(None, 'dp'), may hold values from -6 to 6
- w_in: bfloat16 [8, 4, 512, 512], P('section', None, 'dp'), may hold values from -0.25 to 0.25
- w_out: bfloat16 [8, 4, 512, 512], P('section', None, 'dp'), may hold values from -0.0625 to 0.0625
Outputs:
- new_in: float32 [8, 4, 512, 512], P('section', None, 'dp')
- new_out: float32 [8, 4, 512, 512], P('section', None, 'dp')
The draws below stay inside these ranges and needn't reach their ends.
All inputs are finite; a program needn't handle non-finite values.
Results may differ from the reference program's by a relative error of at most 0.03.
Values may be sent and summed in bfloat16 or wider, within the bound.
A program may use at most 128 MiB of HBM per device.

```python
import math
import jax
import jax.numpy as jnp
from jax import lax

C = 512
L = 4
MICRO = 12
R = 64
SECTIONS = 8
PIXELS = 256
N_DP = 4


def block_levels(own_key, extent, shards, low, top_value):
    level = 1.0
    for position, shards_of in shards:
        heights = jax.random.uniform(jax.random.fold_in(jax.random.fold_in(own_key, 6), position), (shards_of,), jnp.float32, low / len(shards), top_value / len(shards))
        level = level * jnp.repeat(jnp.exp(heights), extent[position] // shards_of).reshape((-1,) + (1,) * (len(extent) - 1 - position))
    return level


def normal_values(stream_key, extent, spread, limit, cuts=(), held_as=jnp.bfloat16):
    level = block_levels(stream_key, extent, cuts, -0.22, 0.18) if cuts else 1.0
    array = jax.random.normal(stream_key, extent, jnp.float32) * spread * level
    return jnp.minimum(jnp.maximum(array, -limit), limit).astype(held_as)


def setup_inputs(seed: int = 0) -> dict:
    splits = jax.random.split(jax.random.key(seed), 5)
    return {
        "images": normal_values(splits[0], (MICRO, PIXELS, C), 1.0, 6.0, ((1, 4),)),
        "cotangent": normal_values(splits[1], (MICRO, PIXELS, C), 1.0, 6.0, ((1, 4),)),
        "w_in": normal_values(splits[2], (SECTIONS, L, C, C), C ** -0.5, 0.25, ((0, 8), (2, 4))),
        "w_out": normal_values(splits[3], (SECTIONS, L, C, C), (16 * C) ** -0.5, 0.0625, ((0, 8), (2, 4))),
    }


def cell_forward(start, first, second):

    def step(value, weights):
        pre = jnp.dot(value, weights[0], preferred_element_type=jnp.float32)
        hidden = (pre * jax.nn.sigmoid(pre)).astype(jnp.bfloat16)
        after = (value.astype(jnp.float32) + jnp.dot(hidden, weights[1], preferred_element_type=jnp.float32)).astype(jnp.bfloat16)
        return (after, value)
    return lax.scan(step, start, (first, second))

def cell_backward(inputs, upstream, first, second):

    def step(grad, pieces):
        value, weight_a, weight_b = pieces
        pre = jnp.dot(value, weight_a, preferred_element_type=jnp.float32)
        sig = jax.nn.sigmoid(pre)
        hidden = (pre * sig).astype(jnp.bfloat16)
        dhidden = jnp.dot(grad, weight_b.T, preferred_element_type=jnp.float32)
        dpre = (dhidden * (sig * (1.0 + pre * (1.0 - sig)))).astype(jnp.bfloat16)
        back = (grad.astype(jnp.float32) + jnp.dot(dpre, weight_a.T, preferred_element_type=jnp.float32)).astype(jnp.bfloat16)
        grad_a = jnp.dot(value.T, dpre, preferred_element_type=jnp.float32)
        grad_b = jnp.dot(hidden.T, grad, preferred_element_type=jnp.float32)
        return (back, (grad_a, grad_b))
    return lax.scan(step, upstream, (inputs, first, second), reverse=True)

def reference(images, cotangent, w_in, w_out):
    start = images.reshape(-1, C)

    def forward(value, weights):
        after, unused = cell_forward(value, weights[0], weights[1])
        return (after, value)
    unused, section_inputs = lax.scan(forward, start, (w_in, w_out))

    def backward(grad, pieces):
        value, first, second = pieces
        unused_out, inputs = cell_forward(value, first, second)
        back, grads = cell_backward(inputs, grad, first, second)
        return (back, grads)
    unused_grad, (grad_in, grad_out) = lax.scan(backward, cotangent.reshape(-1, C), (section_inputs, w_in, w_out), reverse=True)
    rate = 0.1 / math.sqrt(MICRO * R * N_DP)
    return (w_in.astype(jnp.float32) - rate * grad_in, w_out.astype(jnp.float32) - rate * grad_out)
```

```python
import functools
import math

import jax
import jax.numpy as jnp
from jax import lax
from jax.experimental import pallas as pl
from jax.experimental.pallas import tpu as pltpu
from jax.sharding import PartitionSpec as P

MESH = pl.DeviceIdType.MESH
GROUP = 2
ROWS = 128


def kernel(
    n_s, n_d, group, tile, rate,
    img, cot, w_in, w_out, new_in, new_out,
    xs, hs, ds, dps, dys, ysend, dxsend, full_in, full_out, acc, gsend, grecv,
    f_tx, f_rx, b_tx, b_rx, w_tx, w_rx, g_tx, g_rx, e_tx, e_rx,
):
    s, d = lax.axis_index("section"), lax.axis_index("dp")
    layers, wr, width = w_in.shape[1:]
    per = layers // group
    part = img.shape[0]
    rows = group * part
    micro = rows // tile
    micro_part = part // tile
    reps = n_d // group
    stages = n_s * group

    b = lax.rem(d, group)
    even = lax.rem(s, 2) == 0
    half = jnp.where(even, b, group - 1 - b)
    stage = s * group + half
    step_dir = jnp.where(even, 1, -1)
    last = half == group - 1
    head = half == 0
    nxt_s = jnp.where(last, jnp.minimum(s + 1, n_s - 1), s)
    nxt_d = jnp.where(last, d, d + step_dir)
    prv_s = jnp.where(head, jnp.maximum(s - 1, 0), s)
    prv_d = jnp.where(head, d, d - step_dir)
    b_end = 0 if n_s % 2 == 0 else group - 1
    NT = (((1,), (1,)), ((), ()))
    TN = (((0,), (0,)), ((), ()))

    barrier = pltpu.get_barrier_semaphore()
    for o in range(1, n_d):
        pl.semaphore_signal(barrier, inc=1, device_id=(s, lax.rem(d + o, n_d)), device_id_type=MESH)

    @pl.when(s > 0)
    def _():
        pl.semaphore_signal(barrier, inc=1, device_id=(s - 1, d), device_id_type=MESH)

    @pl.when(s < n_s - 1)
    def _():
        pl.semaphore_signal(barrier, inc=1, device_id=(s + 1, d), device_id_type=MESH)

    pl.semaphore_wait(
        barrier, n_d - 1 + jnp.where(s > 0, 1, 0) + jnp.where(s < n_s - 1, 1, 0)
    )

    mats = ((w_in, full_in), (w_out, full_out))

    def half_of(dev):
        bb = lax.rem(dev, group)
        return jnp.where(even, bb, group - 1 - bb)

    def block(i, count):
        return pl.ds(pl.multiple_of(i * count, count), count)

    def weight_copy(mat, k, o, at):
        t = lax.rem(d + o, n_d)
        src, dst = mats[mat]
        return pltpu.make_async_remote_copy(
            src_ref=src.at[0, half_of(t) * per + k],
            dst_ref=dst.at[k, block(at, wr)],
            send_sem=w_tx.at[mat, k, o - 1],
            recv_sem=w_rx.at[mat, k, o - 1],
            device_id=(s, t),
            device_id_type=MESH,
        )

    def extra_copy(which, target_b, at):
        src, dst = ((img, xs.at[0]), (cot, dys.at[per - 1]))[which]
        return pltpu.make_async_remote_copy(
            src_ref=src,
            dst_ref=dst.at[block(at, part)],
            send_sem=e_tx.at[which],
            recv_sem=e_rx.at[which, at],
            device_id=(s, d - b + target_b),
            device_id_type=MESH,
        )

    for k in range(per):
        for mat in range(2):
            for o in range(1, n_d):
                weight_copy(mat, k, o, d).start()
    if group > 1:
        @pl.when((s == 0) & (b != 0))
        def _():
            extra_copy(0, 0, b).start()

        @pl.when((s == n_s - 1) & (b != b_end))
        def _():
            extra_copy(1, b_end, b).start()

    for src, dst in mats:
        for k in range(per):
            dst[k, block(d, wr), :] = src[0, half * per + k]

    @pl.when(stage == 0)
    def _():
        xs[0, pl.ds(0, part), :] = img[...]

    @pl.when(stage == stages - 1)
    def _():
        dys[per - 1, pl.ds(b_end * part, part), :] = cot[...]

    def forward_copy(m):
        return pltpu.make_async_remote_copy(
            src_ref=ysend.at[block(m, tile)],
            dst_ref=xs.at[0, block(m, tile)],
            send_sem=f_tx.at[m],
            recv_sem=f_rx.at[m],
            device_id=(nxt_s, nxt_d),
            device_id_type=MESH,
        )

    def backward_copy(m):
        return pltpu.make_async_remote_copy(
            src_ref=dxsend.at[block(m, tile)],
            dst_ref=dys.at[per - 1, block(m, tile)],
            send_sem=b_tx.at[m],
            recv_sem=b_rx.at[m],
            device_id=(prv_s, prv_d),
            device_id_type=MESH,
        )

    def weights_here(mat, k):
        for o in range(1, n_d):
            weight_copy(mat, k, o, lax.rem(d + n_d - o, n_d)).wait_recv()

    def forward(m, carry):
        at = block(m, tile)

        @pl.when(stage > 0)
        def _():
            forward_copy(m).wait_recv()

        for bb in range(1, group):
            @pl.when((stage == 0) & (m == bb * micro_part))
            def _():
                extra_copy(0, 0, bb).wait_recv()

        for k in range(per):
            @pl.when(m == 0)
            def _():
                weights_here(0, k)

            x = xs[k, at, :]
            pre = jnp.dot(x, full_in[k], preferred_element_type=jnp.float32)
            sig = jax.nn.sigmoid(pre)
            h = (pre * sig).astype(jnp.bfloat16)
            hs[k, at, :] = h
            ds[k, at, :] = sig * (1.0 + pre * (1.0 - sig))

            @pl.when(m == 0)
            def _():
                weights_here(1, k)

            y = (
                x.astype(jnp.float32)
                + jnp.dot(h, full_out[k], preferred_element_type=jnp.float32)
            ).astype(jnp.bfloat16)
            if k + 1 < per:
                xs[k + 1, at, :] = y
            else:
                ysend[at, :] = y

        @pl.when(stage < stages - 1)
        def _():
            forward_copy(m).start()

        return carry

    lax.fori_loop(0, micro, forward, 0)

    def backward(m, carry):
        at = block(m, tile)

        @pl.when(stage < stages - 1)
        def _():
            backward_copy(m).wait_recv()

        for bb in range(group):
            if bb != b_end:
                @pl.when((stage == stages - 1) & (m == bb * micro_part))
                def _():
                    extra_copy(1, b_end, bb).wait_recv()

        for k in reversed(range(per)):
            dy = dys[k, at, :]
            dh = lax.dot_general(dy, full_out[k], NT, preferred_element_type=jnp.float32)
            dp = (dh * ds[k, at, :]).astype(jnp.bfloat16)
            dps[k, at, :] = dp
            dx = (
                dy.astype(jnp.float32)
                + lax.dot_general(dp, full_in[k], NT, preferred_element_type=jnp.float32)
            ).astype(jnp.bfloat16)
            if k > 0:
                dys[k - 1, at, :] = dx
            else:
                dxsend[at, :] = dx

        @pl.when(stage > 0)
        def _():
            backward_copy(m).start()

        return carry

    lax.fori_loop(0, micro, backward, 0)

    rep = d // group

    def grad_copy(mat, k, o):
        t = lax.rem(d + o, n_d)
        layer = half * per + k
        return pltpu.make_async_remote_copy(
            src_ref=gsend.at[mat, k, block(t, wr)],
            dst_ref=grecv.at[mat, rep, layer],
            send_sem=g_tx.at[mat, k, o - 1],
            recv_sem=g_rx.at[mat, rep, layer],
            device_id=(s, t),
            device_id_type=MESH,
        )

    chunk = part
    for k in reversed(range(per)):
        for mat in (1, 0):
            left, right = ((xs, dps), (hs, dys))[mat]
            for c in range(rows // chunk):
                term = lax.dot_general(
                    left[k, pl.ds(c * chunk, chunk), :],
                    right[k, pl.ds(c * chunk, chunk), :],
                    TN, preferred_element_type=jnp.float32,
                )
                if c + 1 < rows // chunk:
                    acc[...] = term if c == 0 else acc[...] + term
                else:
                    total = term if c == 0 else acc[...] + term
                    gsend[mat, k] = total.astype(jnp.bfloat16)
            for o in range(1, n_d):
                grad_copy(mat, k, o).start()
            grecv[mat, rep, half * per + k] = gsend[mat, k, block(d, wr), :]

    for layer in reversed(range(layers)):
        owner_half = layer // per
        for mat in (1, 0):
            for r in range(reps):
                host = r * group + jnp.where(even, owner_half, group - 1 - owner_half)

                @pl.when(host != d)
                def _():
                    pltpu.make_async_remote_copy(
                        src_ref=gsend.at[mat, 0, pl.ds(0, wr)],
                        dst_ref=grecv.at[mat, r, layer],
                        send_sem=g_tx.at[mat, 0, 0],
                        recv_sem=g_rx.at[mat, r, layer],
                        device_id=(s, host),
                        device_id_type=MESH,
                    ).wait_recv()

            total = grecv[mat, 0, layer].astype(jnp.float32)
            for r in range(1, reps):
                total += grecv[mat, r, layer].astype(jnp.float32)
            w, out = ((w_in, new_in), (w_out, new_out))[mat]
            out[0, layer] = w[0, layer].astype(jnp.float32) - rate * total

    for mat in range(2):
        for k in range(per):
            for o in range(1, n_d):
                weight_copy(mat, k, o, d).wait_send()
                grad_copy(mat, k, o).wait_send()
    if group > 1:
        @pl.when((s == 0) & (b != 0))
        def _():
            extra_copy(0, 0, b).wait_send()

        @pl.when((s == n_s - 1) & (b != b_end))
        def _():
            extra_copy(1, b_end, b).wait_send()

    def drain(m, carry):
        @pl.when(stage < stages - 1)
        def _():
            forward_copy(m).wait_send()

        @pl.when(stage > 0)
        def _():
            backward_copy(m).wait_send()

        return carry

    lax.fori_loop(0, micro, drain, 0)


def solution(mesh):
    n_s, n_d = mesh.shape["section"], mesh.shape["dp"]

    def per_device(images, cotangent, w_in, w_out):
        micro, pixels, width = images.shape
        layers, wr = w_in.shape[1:3]
        part = micro * pixels
        group, tile = GROUP, ROWS
        rows, per, reps = group * part, layers // group, n_d // group
        steps = rows // tile
        bf, f32 = jnp.bfloat16, jnp.float32
        rate = 0.1 / math.sqrt(part * n_d)
        dma = pltpu.SemaphoreType.DMA
        vmem = pl.BlockSpec(memory_space=pltpu.VMEM)
        return pl.pallas_call(
            functools.partial(kernel, n_s, n_d, group, tile, rate),
            out_shape=(
                jax.ShapeDtypeStruct(w_in.shape, f32),
                jax.ShapeDtypeStruct(w_out.shape, f32),
            ),
            in_specs=[vmem] * 4,
            out_specs=(vmem, vmem),
            scratch_shapes=[
                pltpu.VMEM((per, rows, width), bf),
                pltpu.VMEM((per, rows, width), bf),
                pltpu.VMEM((per, rows, width), f32),
                pltpu.VMEM((per, rows, width), bf),
                pltpu.VMEM((per, rows, width), bf),
                pltpu.VMEM((rows, width), bf),
                pltpu.VMEM((rows, width), bf),
                pltpu.VMEM((per, width, width), bf),
                pltpu.VMEM((per, width, width), bf),
                pltpu.VMEM((width, width), f32),
                pltpu.VMEM((2, per, width, width), bf),
                pltpu.VMEM((2, reps, layers, wr, width), bf),
                dma((steps,)), dma((steps,)), dma((steps,)), dma((steps,)),
                dma((2, per, n_d - 1)), dma((2, per, n_d - 1)),
                dma((2, per, n_d - 1)), dma((2, reps, layers)),
                dma((2,)), dma((2, group)),
            ],
            compiler_params=pltpu.CompilerParams(
                collective_id=0, has_side_effects=True, vmem_limit_bytes=56 * 1024 * 1024
            ),
            cost_estimate=pl.CostEstimate(
                flops=12 * part * layers * width * width, bytes_accessed=8 << 20, transcendentals=0
            ),
        )(images.reshape(part, width), cotangent.reshape(part, width), w_in, w_out)

    in_specs = (
        P(None, "dp", None),
        P(None, "dp", None),
        P("section", None, "dp", None),
        P("section", None, "dp", None),
    )
    out_specs = (P("section", None, "dp", None), P("section", None, "dp", None))
    return jax.shard_map(
        per_device, mesh=mesh, in_specs=in_specs, out_specs=out_specs, check_vma=False
    )
```

```python
import functools
import math

import jax
import jax.numpy as jnp
from jax import lax
from jax.experimental import pallas as pl
from jax.experimental.pallas import tpu as pltpu
from jax.sharding import PartitionSpec as P

MESH = pl.DeviceIdType.MESH
GROUP = 2
ROWS = 64


def kernel(
    n_s, n_d, group, tile, rate,
    img, cot, w_in, w_out, new_in, new_out,
    left, right, ds, ysend, dxsend, full, acc, gsend, gpeer, gtotal, grecv,
    f_tx, f_rx, b_tx, b_rx, w_tx, w_rx, p_tx, g_tx, g_rx, x_tx, x_rx, e_tx, e_rx,
):
    s, d = lax.axis_index("section"), lax.axis_index("dp")
    layers, wr, width = w_in.shape[1:]
    per = 2 * layers // group
    part = img.shape[0]
    share = group // 2
    rows = share * part
    micro = rows // tile
    micro_part = part // tile
    reps = n_d // group
    columns = n_s // 2
    stages = columns * group

    col, core = s // 2, lax.rem(s, 2)
    mate = 2 * col + 1 - core
    b = lax.rem(d, group)
    base = d - b
    rep = d // group
    even = lax.rem(col, 2) == 0
    half = jnp.where(even, b, group - 1 - b)
    stage = col * group + half
    step_dir = jnp.where(even, 1, -1)
    last = half == group - 1
    head = half == 0
    nxt_s = jnp.where(last, jnp.minimum(s + 2, n_s - 2 + core), s)
    nxt_d = jnp.where(last, d, d + step_dir)
    prv_s = jnp.where(head, jnp.maximum(s - 2, core), s)
    prv_d = jnp.where(head, d, d - step_dir)
    b_end = 0 if columns % 2 == 0 else group - 1
    NT = (((1,), (1,)), ((), ()))
    TN = (((0,), (0,)), ((), ()))

    barrier = pltpu.get_barrier_semaphore()
    pl.semaphore_signal(barrier, inc=1, device_id=(mate, d), device_id_type=MESH)
    for o in range(1, n_d):
        for cc in range(2):
            pl.semaphore_signal(
                barrier, inc=1, device_id=(2 * col + cc, lax.rem(d + o, n_d)), device_id_type=MESH
            )

    @pl.when(col > 0)
    def _():
        pl.semaphore_signal(barrier, inc=1, device_id=(s - 2, d), device_id_type=MESH)

    @pl.when(col < columns - 1)
    def _():
        pl.semaphore_signal(barrier, inc=1, device_id=(s + 2, d), device_id_type=MESH)

    pl.semaphore_wait(
        barrier,
        2 * n_d - 1 + jnp.where(col > 0, 1, 0) + jnp.where(col < columns - 1, 1, 0),
    )

    def host(r, h):
        return r * group + jnp.where(even, h, group - 1 - h)

    def block(i, count):
        return pl.ds(pl.multiple_of(i * count, count), count)

    def weight_copy(mat, layer, r):
        t = host(r, (core * layers + layer) // per)
        return pltpu.make_async_remote_copy(
            src_ref=(w_in, w_out)[mat].at[0, layer],
            dst_ref=full.at[mat, layer % per, block(d, wr)],
            send_sem=w_tx.at[mat, layer, r],
            recv_sem=w_rx.at[mat, layer % per, d],
            device_id=(jnp.where(t == d, mate, 2 * col + mat), t),
            device_id_type=MESH,
        )

    def pass_copy(mat, k, zz, slot):
        ref = full.at[mat, k, block(zz, wr)]
        return pltpu.make_async_remote_copy(
            src_ref=ref,
            dst_ref=ref,
            send_sem=p_tx.at[k, slot],
            recv_sem=w_rx.at[mat, k, zz],
            device_id=(mate, d),
            device_id_type=MESH,
        )

    def extra_copy(which, target_b, at):
        src, dst = ((img, left.at[0, 0]), (cot, right.at[1, per - 1]))[which]
        return pltpu.make_async_remote_copy(
            src_ref=src,
            dst_ref=dst.at[block(at, part)],
            send_sem=e_tx.at[which],
            recv_sem=e_rx.at[which, at],
            device_id=(s, base + target_b),
            device_id_type=MESH,
        )

    feeds = (b // share) == core
    feed_in = (col == 0) & (b != 0) & feeds
    feed_out = (col == columns - 1) & (b != b_end) & feeds
    slot_of = lax.rem(b, share)

    @pl.when(feed_in)
    def _():
        extra_copy(0, 0, slot_of).start()

    for layer in range(layers):
        for mat in range(2):
            for r in range(reps):
                weight_copy(mat, layer, r).start()

    @pl.when(feed_out)
    def _():
        extra_copy(1, b_end, slot_of).start()

    for k in range(per):
        e = half * per + k

        @pl.when(e // layers == core)
        def _():
            full[0, k, block(d, wr), :] = w_in[0, lax.rem(e, layers)]
            full[1, k, block(d, wr), :] = w_out[0, lax.rem(e, layers)]

    @pl.when((stage == 0) & (core == 0))
    def _():
        left[0, 0, pl.ds(0, part), :] = img[...]

    @pl.when((stage == stages - 1) & (core == b_end // share))
    def _():
        right[1, per - 1, pl.ds((b_end % share) * part, part), :] = cot[...]

    def forward_copy(m):
        return pltpu.make_async_remote_copy(
            src_ref=ysend.at[block(m, tile)],
            dst_ref=left.at[0, 0, block(m, tile)],
            send_sem=f_tx.at[m],
            recv_sem=f_rx.at[m],
            device_id=(nxt_s, nxt_d),
            device_id_type=MESH,
        )

    def backward_copy(m):
        return pltpu.make_async_remote_copy(
            src_ref=dxsend.at[block(m, tile)],
            dst_ref=right.at[1, per - 1, block(m, tile)],
            send_sem=b_tx.at[m],
            recv_sem=b_rx.at[m],
            device_id=(prv_s, prv_d),
            device_id_type=MESH,
        )

    def weights_here(k):
        for o in range(1, n_d):
            zz = lax.rem(d + o, n_d)
            arrived = pass_copy(core, k, zz, o - 1)
            arrived.wait_recv()
            arrived.start()

        @pl.when((half * per + k) // layers != core)
        def _():
            pass_copy(0, k, d, 0).wait_recv()
            pass_copy(1, k, d, 0).wait_recv()

        for o in range(1, n_d):
            pass_copy(1 - core, k, lax.rem(d + o, n_d), o - 1).wait_recv()

    @pl.when(stage > 0)
    def _():
        for k in range(per):
            weights_here(k)

    def forward(m, carry):
        at = block(m, tile)

        @pl.when(stage > 0)
        def _():
            forward_copy(m).wait_recv()

        for i in range(share):
            for cc in range(2):
                if i + cc > 0:
                    @pl.when((stage == 0) & (core == cc) & (m == i * micro_part))
                    def _():
                        extra_copy(0, 0, i).wait_recv()

        for k in range(per):
            @pl.when((stage == 0) & (m == 0))
            def _():
                weights_here(k)

            x = left[0, k, at, :]
            pre = jnp.dot(x, full[0, k], preferred_element_type=jnp.float32)
            sig = jax.nn.sigmoid(pre)
            h = (pre * sig).astype(jnp.bfloat16)
            left[1, k, at, :] = h
            ds[k, at, :] = sig * (1.0 + pre * (1.0 - sig))
            y = (
                x.astype(jnp.float32)
                + jnp.dot(h, full[1, k], preferred_element_type=jnp.float32)
            ).astype(jnp.bfloat16)
            if k + 1 < per:
                left[0, k + 1, at, :] = y
            else:
                ysend[at, :] = y

        @pl.when(stage < stages - 1)
        def _():
            forward_copy(m).start()

        return carry

    lax.fori_loop(0, micro, forward, 0)

    def backward(m, carry):
        at = block(m, tile)

        @pl.when(stage < stages - 1)
        def _():
            backward_copy(m).wait_recv()

        for i in range(share):
            for cc in range(2):
                if cc * share + i != b_end:
                    @pl.when((stage == stages - 1) & (core == cc) & (m == i * micro_part))
                    def _():
                        extra_copy(1, b_end, i).wait_recv()

        for k in reversed(range(per)):
            dy = right[1, k, at, :]
            dh = lax.dot_general(dy, full[1, k], NT, preferred_element_type=jnp.float32)
            dp = (dh * ds[k, at, :]).astype(jnp.bfloat16)
            right[0, k, at, :] = dp
            dx = (
                dy.astype(jnp.float32)
                + lax.dot_general(dp, full[0, k], NT, preferred_element_type=jnp.float32)
            ).astype(jnp.bfloat16)
            if k > 0:
                right[1, k - 1, at, :] = dx
            else:
                dxsend[at, :] = dx

        @pl.when(stage > 0)
        def _():
            backward_copy(m).start()

        return carry

    lax.fori_loop(0, micro, backward, 0)

    def swap_copy(k):
        return pltpu.make_async_remote_copy(
            src_ref=gsend.at[k],
            dst_ref=gpeer.at[k],
            send_sem=x_tx.at[k],
            recv_sem=x_rx.at[k],
            device_id=(mate, d),
            device_id_type=MESH,
        )

    def grad_copy(k, t, slot):
        e = half * per + k
        return pltpu.make_async_remote_copy(
            src_ref=gtotal.at[k, block(t, wr)],
            dst_ref=grecv.at[core, rep, lax.rem(e, layers)],
            send_sem=g_tx.at[k, slot],
            recv_sem=g_rx.at[core, rep, lax.rem(e, layers)],
            device_id=(2 * col + e // layers, t),
            device_id_type=MESH,
        )

    def product(mat, k):
        for c in range(share):
            at = pl.ds(c * part, part)
            term = lax.dot_general(
                left[mat, k, at, :], right[mat, k, at, :], TN, preferred_element_type=jnp.float32
            )
            acc[...] = term if c == 0 else acc[...] + term

    for k in reversed(range(per)):
        e = half * per + k
        product(1 - core, k)
        gsend[k] = acc[...].astype(jnp.bfloat16)
        swap_copy(k).start()
        product(core, k)
        swap_copy(k).wait_recv()
        gtotal[k] = (acc[...] + gpeer[k].astype(jnp.float32)).astype(jnp.bfloat16)
        for o in range(1, n_d):
            grad_copy(k, lax.rem(d + o, n_d), o).start()

        @pl.when(e // layers != core)
        def _():
            grad_copy(k, d, 0).start()

        @pl.when(e // layers == core)
        def _():
            grecv[core, rep, lax.rem(e, layers)] = gtotal[k, block(d, wr), :]

    for layer in reversed(range(layers)):
        for mat in (1, 0):
            for r in range(reps):
                t = host(r, (core * layers + layer) // per)

                @pl.when((t != d) | (core != mat))
                def _():
                    pltpu.make_async_remote_copy(
                        src_ref=gtotal.at[0, pl.ds(0, wr)],
                        dst_ref=grecv.at[mat, r, layer],
                        send_sem=g_tx.at[0, 0],
                        recv_sem=g_rx.at[mat, r, layer],
                        device_id=(mate, d),
                        device_id_type=MESH,
                    ).wait_recv()

            total = grecv[mat, 0, layer].astype(jnp.float32)
            for r in range(1, reps):
                total += grecv[mat, r, layer].astype(jnp.float32)
            w, out = ((w_in, new_in), (w_out, new_out))[mat]
            out[0, layer] = w[0, layer].astype(jnp.float32) - rate * total

    for layer in range(layers):
        for mat in range(2):
            for r in range(reps):
                weight_copy(mat, layer, r).wait_send()
    for k in range(per):
        e = half * per + k
        swap_copy(k).wait_send()
        for o in range(1, n_d):
            pass_copy(core, k, lax.rem(d + o, n_d), o - 1).wait_send()
            grad_copy(k, lax.rem(d + o, n_d), o).wait_send()

        @pl.when(e // layers != core)
        def _():
            grad_copy(k, d, 0).wait_send()

    @pl.when(feed_in)
    def _():
        extra_copy(0, 0, slot_of).wait_send()

    @pl.when(feed_out)
    def _():
        extra_copy(1, b_end, slot_of).wait_send()

    def drain(m, carry):
        @pl.when(stage < stages - 1)
        def _():
            forward_copy(m).wait_send()

        @pl.when(stage > 0)
        def _():
            backward_copy(m).wait_send()

        return carry

    lax.fori_loop(0, micro, drain, 0)


def solution(mesh):
    n_s, n_d = mesh.shape["section"], mesh.shape["dp"]

    def per_device(images, cotangent, w_in, w_out):
        micro, pixels, width = images.shape
        layers, wr = w_in.shape[1:3]
        part = micro * pixels
        group, tile = GROUP, ROWS
        rows, per, reps = group // 2 * part, 2 * layers // group, n_d // group
        steps = rows // tile
        bf, f32 = jnp.bfloat16, jnp.float32
        rate = 0.1 / math.sqrt(part * n_d)
        dma = pltpu.SemaphoreType.DMA
        vmem = pl.BlockSpec(memory_space=pltpu.VMEM)
        return pl.pallas_call(
            functools.partial(kernel, n_s, n_d, group, tile, rate),
            out_shape=(
                jax.ShapeDtypeStruct(w_in.shape, f32),
                jax.ShapeDtypeStruct(w_out.shape, f32),
            ),
            in_specs=[vmem] * 4,
            out_specs=(vmem, vmem),
            scratch_shapes=[
                pltpu.VMEM((2, per, rows, width), bf),
                pltpu.VMEM((2, per, rows, width), bf),
                pltpu.VMEM((per, rows, width), f32),
                pltpu.VMEM((rows, width), bf),
                pltpu.VMEM((rows, width), bf),
                pltpu.VMEM((2, per, width, width), bf),
                pltpu.VMEM((width, width), f32),
                pltpu.VMEM((per, width, width), bf),
                pltpu.VMEM((per, width, width), bf),
                pltpu.VMEM((per, width, width), bf),
                pltpu.VMEM((2, reps, layers, wr, width), bf),
                dma((steps,)), dma((steps,)), dma((steps,)), dma((steps,)),
                dma((2, layers, reps)), dma((2, per, n_d)), dma((per, n_d - 1)),
                dma((per, n_d)), dma((2, reps, layers)),
                dma((per,)), dma((per,)),
                dma((2,)), dma((2, group // 2)),
            ],
            compiler_params=pltpu.CompilerParams(
                collective_id=0, has_side_effects=True, vmem_limit_bytes=56 * 1024 * 1024
            ),
            cost_estimate=pl.CostEstimate(
                flops=12 * part * layers * width * width, bytes_accessed=8 << 20, transcendentals=0
            ),
        )(images.reshape(part, width), cotangent.reshape(part, width), w_in, w_out)

    in_specs = (
        P(None, "dp", None),
        P(None, "dp", None),
        P("section", None, "dp", None),
        P("section", None, "dp", None),
    )
    out_specs = (P("section", None, "dp", None), P("section", None, "dp", None))
    return jax.shard_map(
        per_device, mesh=mesh, in_specs=in_specs, out_specs=out_specs, check_vma=False
    )
```

```python
import functools
import math

import jax
import jax.numpy as jnp
from jax import lax
from jax.experimental import pallas as pl
from jax.experimental.pallas import tpu as pltpu
from jax.sharding import PartitionSpec as P

MESH = pl.DeviceIdType.MESH
GROUP = 2
ROWS = 64


def kernel(
    n_s, n_d, group, tile, rate,
    img, cot, w_in, w_out, new_in, new_out,
    left, right, ds, ysend, dxsend, full, full_t, acc, gsend, gpeer, gtotal, grecv,
    f_tx, f_rx, b_tx, b_rx, w_tx, w_rx, p_tx, g_tx, g_rx, x_tx, x_rx, e_tx, e_rx,
):
    s, d = lax.axis_index("section"), lax.axis_index("dp")
    layers, wr, width = w_in.shape[1:]
    per = 2 * layers // group
    part = img.shape[0]
    share = group // 2
    rows = share * part
    micro = rows // tile
    micro_part = part // tile
    reps = n_d // group
    columns = n_s // 2
    stages = columns * group

    col, core = s // 2, lax.rem(s, 2)
    mate = 2 * col + 1 - core
    b = lax.rem(d, group)
    base = d - b
    rep = d // group
    even = lax.rem(col, 2) == 0
    half = jnp.where(even, b, group - 1 - b)
    stage = col * group + half
    step_dir = jnp.where(even, 1, -1)
    last = half == group - 1
    head = half == 0
    nxt_s = jnp.where(last, jnp.minimum(s + 2, n_s - 2 + core), s)
    nxt_d = jnp.where(last, d, d + step_dir)
    prv_s = jnp.where(head, jnp.maximum(s - 2, core), s)
    prv_d = jnp.where(head, d, d - step_dir)
    b_end = 0 if columns % 2 == 0 else group - 1
    TN = (((0,), (0,)), ((), ()))

    barrier = pltpu.get_barrier_semaphore()
    pl.semaphore_signal(barrier, inc=1, device_id=(mate, d), device_id_type=MESH)
    for o in range(1, n_d):
        for cc in range(2):
            pl.semaphore_signal(
                barrier, inc=1, device_id=(2 * col + cc, lax.rem(d + o, n_d)), device_id_type=MESH
            )

    @pl.when(col > 0)
    def _():
        pl.semaphore_signal(barrier, inc=1, device_id=(s - 2, d), device_id_type=MESH)

    @pl.when(col < columns - 1)
    def _():
        pl.semaphore_signal(barrier, inc=1, device_id=(s + 2, d), device_id_type=MESH)

    pl.semaphore_wait(
        barrier,
        2 * n_d - 1 + jnp.where(col > 0, 1, 0) + jnp.where(col < columns - 1, 1, 0),
    )

    def host(r, h):
        return r * group + jnp.where(even, h, group - 1 - h)

    def block(i, count):
        return pl.ds(pl.multiple_of(i * count, count), count)

    def weight_copy(mat, layer, r):
        t = host(r, (core * layers + layer) // per)
        return pltpu.make_async_remote_copy(
            src_ref=(w_in, w_out)[mat].at[0, layer],
            dst_ref=full.at[mat, layer % per, block(d, wr)],
            send_sem=w_tx.at[mat, layer, r],
            recv_sem=w_rx.at[mat, layer % per, d],
            device_id=(jnp.where(t == d, mate, 2 * col + mat), t),
            device_id_type=MESH,
        )

    def pass_copy(mat, k, zz, slot):
        ref = full.at[mat, k, block(zz, wr)]
        return pltpu.make_async_remote_copy(
            src_ref=ref,
            dst_ref=ref,
            send_sem=p_tx.at[k, slot],
            recv_sem=w_rx.at[mat, k, zz],
            device_id=(mate, d),
            device_id_type=MESH,
        )

    def extra_copy(which, target_b, at):
        src, dst = ((img, left.at[0, 0]), (cot, right.at[1, per - 1]))[which]
        return pltpu.make_async_remote_copy(
            src_ref=src,
            dst_ref=dst.at[block(at, part)],
            send_sem=e_tx.at[which],
            recv_sem=e_rx.at[which, at],
            device_id=(s, base + target_b),
            device_id_type=MESH,
        )

    feeds = (b // share) == core
    feed_in = (col == 0) & (b != 0) & feeds
    feed_out = (col == columns - 1) & (b != b_end) & feeds
    slot_of = lax.rem(b, share)

    @pl.when(feed_in)
    def _():
        extra_copy(0, 0, slot_of).start()

    for layer in range(layers):
        for mat in range(2):
            for r in range(reps):
                weight_copy(mat, layer, r).start()

    @pl.when(feed_out)
    def _():
        extra_copy(1, b_end, slot_of).start()

    for k in range(per):
        e = half * per + k

        @pl.when(e // layers == core)
        def _():
            full[0, k, block(d, wr), :] = w_in[0, lax.rem(e, layers)]
            full[1, k, block(d, wr), :] = w_out[0, lax.rem(e, layers)]

    @pl.when((stage == 0) & (core == 0))
    def _():
        left[0, 0, pl.ds(0, part), :] = img[...]

    @pl.when((stage == stages - 1) & (core == b_end // share))
    def _():
        right[1, per - 1, pl.ds((b_end % share) * part, part), :] = cot[...]

    def forward_copy(m):
        return pltpu.make_async_remote_copy(
            src_ref=ysend.at[block(m, tile)],
            dst_ref=left.at[0, 0, block(m, tile)],
            send_sem=f_tx.at[m],
            recv_sem=f_rx.at[m],
            device_id=(nxt_s, nxt_d),
            device_id_type=MESH,
        )

    def backward_copy(m):
        return pltpu.make_async_remote_copy(
            src_ref=dxsend.at[block(m, tile)],
            dst_ref=right.at[1, per - 1, block(m, tile)],
            send_sem=b_tx.at[m],
            recv_sem=b_rx.at[m],
            device_id=(prv_s, prv_d),
            device_id_type=MESH,
        )

    def weights_here(k):
        for o in range(1, n_d):
            zz = lax.rem(d + o, n_d)
            arrived = pass_copy(core, k, zz, o - 1)
            arrived.wait_recv()
            arrived.start()

        @pl.when((half * per + k) // layers != core)
        def _():
            pass_copy(0, k, d, 0).wait_recv()
            pass_copy(1, k, d, 0).wait_recv()

        for o in range(1, n_d):
            pass_copy(1 - core, k, lax.rem(d + o, n_d), o - 1).wait_recv()

    @pl.when(stage > 0)
    def _():
        for k in range(per):
            weights_here(k)

    def forward(m, carry):
        at = block(m, tile)

        @pl.when(stage > 0)
        def _():
            forward_copy(m).wait_recv()

        for i in range(share):
            for cc in range(2):
                if i + cc > 0:
                    @pl.when((stage == 0) & (core == cc) & (m == i * micro_part))
                    def _():
                        extra_copy(0, 0, i).wait_recv()

        for k in range(per):
            @pl.when((stage == 0) & (m == 0))
            def _():
                weights_here(k)

            x = left[0, k, at, :]
            pre = jnp.dot(x, full[0, k], preferred_element_type=jnp.float32)
            sig = jax.nn.sigmoid(pre)
            h = (pre * sig).astype(jnp.bfloat16)
            left[1, k, at, :] = h
            ds[k, at, :] = sig * (1.0 + pre * (1.0 - sig))
            y = (
                x.astype(jnp.float32)
                + jnp.dot(h, full[1, k], preferred_element_type=jnp.float32)
            ).astype(jnp.bfloat16)
            if k + 1 < per:
                left[0, k + 1, at, :] = y
            else:
                ysend[at, :] = y

        @pl.when(stage < stages - 1)
        def _():
            forward_copy(m).start()

        return carry

    def transpose_weights():
        for mat in range(2):
            for k in range(per):
                full_t[mat, k] = full[mat, k].T

    @pl.when(stage >= stages // 2)
    def _():
        transpose_weights()

    lax.fori_loop(0, micro, forward, 0)

    @pl.when(stage < stages // 2)
    def _():
        transpose_weights()

    def backward(m, carry):
        at = block(m, tile)

        @pl.when(stage < stages - 1)
        def _():
            backward_copy(m).wait_recv()

        for i in range(share):
            for cc in range(2):
                if cc * share + i != b_end:
                    @pl.when((stage == stages - 1) & (core == cc) & (m == i * micro_part))
                    def _():
                        extra_copy(1, b_end, i).wait_recv()

        for k in reversed(range(per)):
            dy = right[1, k, at, :]
            dh = jnp.dot(dy, full_t[1, k], preferred_element_type=jnp.float32)
            dp = (dh * ds[k, at, :]).astype(jnp.bfloat16)
            right[0, k, at, :] = dp
            dx = (
                dy.astype(jnp.float32)
                + jnp.dot(dp, full_t[0, k], preferred_element_type=jnp.float32)
            ).astype(jnp.bfloat16)
            if k > 0:
                right[1, k - 1, at, :] = dx
            else:
                dxsend[at, :] = dx

        @pl.when(stage > 0)
        def _():
            backward_copy(m).start()

        return carry

    lax.fori_loop(0, micro, backward, 0)

    def swap_copy(k):
        return pltpu.make_async_remote_copy(
            src_ref=gsend.at[k],
            dst_ref=gpeer.at[k],
            send_sem=x_tx.at[k],
            recv_sem=x_rx.at[k],
            device_id=(mate, d),
            device_id_type=MESH,
        )

    def grad_copy(k, t, slot):
        e = half * per + k
        return pltpu.make_async_remote_copy(
            src_ref=gtotal.at[k, block(t, wr)],
            dst_ref=grecv.at[core, rep, lax.rem(e, layers)],
            send_sem=g_tx.at[k, slot],
            recv_sem=g_rx.at[core, rep, lax.rem(e, layers)],
            device_id=(2 * col + e // layers, t),
            device_id_type=MESH,
        )

    def product(mat, k):
        for c in range(share):
            at = pl.ds(c * part, part)
            term = lax.dot_general(
                left[mat, k, at, :], right[mat, k, at, :], TN, preferred_element_type=jnp.float32
            )
            acc[...] = term if c == 0 else acc[...] + term

    for k in reversed(range(per)):
        e = half * per + k
        product(1 - core, k)
        gsend[k] = acc[...].astype(jnp.bfloat16)
        swap_copy(k).start()
        product(core, k)
        swap_copy(k).wait_recv()
        gtotal[k] = (acc[...] + gpeer[k].astype(jnp.float32)).astype(jnp.bfloat16)
        for o in range(1, n_d):
            grad_copy(k, lax.rem(d + o, n_d), o).start()

        @pl.when(e // layers != core)
        def _():
            grad_copy(k, d, 0).start()

        @pl.when(e // layers == core)
        def _():
            grecv[core, rep, lax.rem(e, layers)] = gtotal[k, block(d, wr), :]

    for layer in reversed(range(layers)):
        for mat in (1, 0):
            for r in range(reps):
                t = host(r, (core * layers + layer) // per)

                @pl.when((t != d) | (core != mat))
                def _():
                    pltpu.make_async_remote_copy(
                        src_ref=gtotal.at[0, pl.ds(0, wr)],
                        dst_ref=grecv.at[mat, r, layer],
                        send_sem=g_tx.at[0, 0],
                        recv_sem=g_rx.at[mat, r, layer],
                        device_id=(mate, d),
                        device_id_type=MESH,
                    ).wait_recv()

            total = grecv[mat, 0, layer].astype(jnp.float32)
            for r in range(1, reps):
                total += grecv[mat, r, layer].astype(jnp.float32)
            w, out = ((w_in, new_in), (w_out, new_out))[mat]
            out[0, layer] = w[0, layer].astype(jnp.float32) - rate * total

    for layer in range(layers):
        for mat in range(2):
            for r in range(reps):
                weight_copy(mat, layer, r).wait_send()
    for k in range(per):
        e = half * per + k
        swap_copy(k).wait_send()
        for o in range(1, n_d):
            pass_copy(core, k, lax.rem(d + o, n_d), o - 1).wait_send()
            grad_copy(k, lax.rem(d + o, n_d), o).wait_send()

        @pl.when(e // layers != core)
        def _():
            grad_copy(k, d, 0).wait_send()

    @pl.when(feed_in)
    def _():
        extra_copy(0, 0, slot_of).wait_send()

    @pl.when(feed_out)
    def _():
        extra_copy(1, b_end, slot_of).wait_send()

    def drain(m, carry):
        @pl.when(stage < stages - 1)
        def _():
            forward_copy(m).wait_send()

        @pl.when(stage > 0)
        def _():
            backward_copy(m).wait_send()

        return carry

    lax.fori_loop(0, micro, drain, 0)


def solution(mesh):
    n_s, n_d = mesh.shape["section"], mesh.shape["dp"]

    def per_device(images, cotangent, w_in, w_out):
        micro, pixels, width = images.shape
        layers, wr = w_in.shape[1:3]
        part = micro * pixels
        group, tile = GROUP, ROWS
        rows, per, reps = group // 2 * part, 2 * layers // group, n_d // group
        steps = rows // tile
        bf, f32 = jnp.bfloat16, jnp.float32
        rate = 0.1 / math.sqrt(part * n_d)
        dma = pltpu.SemaphoreType.DMA
        vmem = pl.BlockSpec(memory_space=pltpu.VMEM)
        return pl.pallas_call(
            functools.partial(kernel, n_s, n_d, group, tile, rate),
            out_shape=(
                jax.ShapeDtypeStruct(w_in.shape, f32),
                jax.ShapeDtypeStruct(w_out.shape, f32),
            ),
            in_specs=[vmem] * 4,
            out_specs=(vmem, vmem),
            scratch_shapes=[
                pltpu.VMEM((2, per, rows, width), bf),
                pltpu.VMEM((2, per, rows, width), bf),
                pltpu.VMEM((per, rows, width), f32),
                pltpu.VMEM((rows, width), bf),
                pltpu.VMEM((rows, width), bf),
                pltpu.VMEM((2, per, width, width), bf),
                pltpu.VMEM((2, per, width, width), bf),
                pltpu.VMEM((width, width), f32),
                pltpu.VMEM((per, width, width), bf),
                pltpu.VMEM((per, width, width), bf),
                pltpu.VMEM((per, width, width), bf),
                pltpu.VMEM((2, reps, layers, wr, width), bf),
                dma((steps,)), dma((steps,)), dma((steps,)), dma((steps,)),
                dma((2, layers, reps)), dma((2, per, n_d)), dma((per, n_d - 1)),
                dma((per, n_d)), dma((2, reps, layers)),
                dma((per,)), dma((per,)),
                dma((2,)), dma((2, group // 2)),
            ],
            compiler_params=pltpu.CompilerParams(
                collective_id=0, has_side_effects=True, vmem_limit_bytes=56 * 1024 * 1024
            ),
            cost_estimate=pl.CostEstimate(
                flops=12 * part * layers * width * width, bytes_accessed=8 << 20, transcendentals=0
            ),
        )(images.reshape(part, width), cotangent.reshape(part, width), w_in, w_out)

    in_specs = (
        P(None, "dp", None),
        P(None, "dp", None),
        P("section", None, "dp", None),
        P("section", None, "dp", None),
    )
    out_specs = (P("section", None, "dp", None), P("section", None, "dp", None))
    return jax.shard_map(
        per_device, mesh=mesh, in_specs=in_specs, out_specs=out_specs, check_vma=False
    )
```

```python
import functools
import math

import jax
import jax.numpy as jnp
from jax import lax
from jax.experimental import pallas as pl
from jax.experimental.pallas import tpu as pltpu
from jax.sharding import PartitionSpec as P

MESH = pl.DeviceIdType.MESH
GROUP = 2
ROWS = 64


def kernel(
    n_s, n_d, group, tile, rate,
    img, cot, w_in, w_out, new_in, new_out,
    left, right, ds, ysend, dxsend, full, full_t, acc, gsend, gpeer, gtotal, grecv,
    f_tx, f_rx, b_tx, b_rx, w_tx, w_rx, p_tx, g_tx, g_rx, x_tx, x_rx, e_tx, e_rx,
):
    s, d = lax.axis_index("section"), lax.axis_index("dp")
    layers, wr, width = w_in.shape[1:]
    per = 2 * layers // group
    part = img.shape[0]
    share = group // 2
    rows = share * part
    micro = rows // tile
    micro_part = part // tile
    reps = n_d // group
    columns = n_s // 2
    stages = columns * group

    col, core = s // 2, lax.rem(s, 2)
    mate = 2 * col + 1 - core
    b = lax.rem(d, group)
    base = d - b
    rep = d // group
    even = lax.rem(col, 2) == 0
    half = jnp.where(even, b, group - 1 - b)
    stage = col * group + half
    step_dir = jnp.where(even, 1, -1)
    last = half == group - 1
    head = half == 0
    nxt_s = jnp.where(last, jnp.minimum(s + 2, n_s - 2 + core), s)
    nxt_d = jnp.where(last, d, d + step_dir)
    prv_s = jnp.where(head, jnp.maximum(s - 2, core), s)
    prv_d = jnp.where(head, d, d - step_dir)
    b_end = 0 if columns % 2 == 0 else group - 1
    TN = (((0,), (0,)), ((), ()))

    barrier = pltpu.get_barrier_semaphore()
    pl.semaphore_signal(barrier, inc=1, device_id=(mate, d), device_id_type=MESH)
    for o in range(1, n_d):
        for cc in range(2):
            pl.semaphore_signal(
                barrier, inc=1, device_id=(2 * col + cc, lax.rem(d + o, n_d)), device_id_type=MESH
            )

    @pl.when(col > 0)
    def _():
        pl.semaphore_signal(barrier, inc=1, device_id=(s - 2, d), device_id_type=MESH)

    @pl.when(col < columns - 1)
    def _():
        pl.semaphore_signal(barrier, inc=1, device_id=(s + 2, d), device_id_type=MESH)

    pl.semaphore_wait(
        barrier,
        2 * n_d - 1 + jnp.where(col > 0, 1, 0) + jnp.where(col < columns - 1, 1, 0),
    )

    def host(r, h):
        return r * group + jnp.where(even, h, group - 1 - h)

    def block(i, count):
        return pl.ds(pl.multiple_of(i * count, count), count)

    def weight_copy(mat, layer, r):
        t = host(r, (core * layers + layer) // per)
        return pltpu.make_async_remote_copy(
            src_ref=(w_in, w_out)[mat].at[0, layer],
            dst_ref=full.at[mat, layer % per, block(d, wr)],
            send_sem=w_tx.at[mat, layer, r],
            recv_sem=w_rx.at[mat, layer % per, d],
            device_id=(jnp.where(t == d, mate, 2 * col + mat), t),
            device_id_type=MESH,
        )

    def pass_copy(mat, k, zz, slot):
        ref = full.at[mat, k, block(zz, wr)]
        return pltpu.make_async_remote_copy(
            src_ref=ref,
            dst_ref=ref,
            send_sem=p_tx.at[k, slot],
            recv_sem=w_rx.at[mat, k, zz],
            device_id=(mate, d),
            device_id_type=MESH,
        )

    def extra_copy(which, target_b, at):
        src, dst = ((img, left.at[0, 0]), (cot, right.at[1, per - 1]))[which]
        return pltpu.make_async_remote_copy(
            src_ref=src,
            dst_ref=dst.at[block(at, part)],
            send_sem=e_tx.at[which],
            recv_sem=e_rx.at[which, at],
            device_id=(s, base + target_b),
            device_id_type=MESH,
        )

    feeds = (b // share) == core
    feed_in = (col == 0) & (b != 0) & feeds
    feed_out = (col == columns - 1) & (b != b_end) & feeds
    slot_of = lax.rem(b, share)

    @pl.when(feed_in)
    def _():
        extra_copy(0, 0, slot_of).start()

    for layer in range(layers):
        for mat in range(2):
            for r in range(1, reps + 1):
                weight_copy(mat, layer, lax.rem(rep + r, reps)).start()

    @pl.when(feed_out)
    def _():
        extra_copy(1, b_end, slot_of).start()

    for k in range(per):
        e = half * per + k

        @pl.when(e // layers == core)
        def _():
            full[0, k, block(d, wr), :] = w_in[0, lax.rem(e, layers)]
            full[1, k, block(d, wr), :] = w_out[0, lax.rem(e, layers)]

    @pl.when((stage == 0) & (core == 0))
    def _():
        left[0, 0, pl.ds(0, part), :] = img[...]

    @pl.when((stage == stages - 1) & (core == b_end // share))
    def _():
        right[1, per - 1, pl.ds((b_end % share) * part, part), :] = cot[...]

    def forward_copy(m):
        return pltpu.make_async_remote_copy(
            src_ref=ysend.at[block(m, tile)],
            dst_ref=left.at[0, 0, block(m, tile)],
            send_sem=f_tx.at[m],
            recv_sem=f_rx.at[m],
            device_id=(nxt_s, nxt_d),
            device_id_type=MESH,
        )

    def backward_copy(m):
        return pltpu.make_async_remote_copy(
            src_ref=dxsend.at[block(m, tile)],
            dst_ref=right.at[1, per - 1, block(m, tile)],
            send_sem=b_tx.at[m],
            recv_sem=b_rx.at[m],
            device_id=(prv_s, prv_d),
            device_id_type=MESH,
        )

    def weights_here(k):
        for o in range(1, n_d):
            zz = lax.rem(d + o, n_d)
            arrived = pass_copy(core, k, zz, o - 1)
            arrived.wait_recv()
            arrived.start()

        @pl.when((half * per + k) // layers != core)
        def _():
            pass_copy(0, k, d, 0).wait_recv()
            pass_copy(1, k, d, 0).wait_recv()

        for o in range(1, n_d):
            pass_copy(1 - core, k, lax.rem(d + o, n_d), o - 1).wait_recv()

    @pl.when(stage > 0)
    def _():
        for k in range(per):
            weights_here(k)

    def forward(m, carry):
        at = block(m, tile)

        @pl.when(stage > 0)
        def _():
            forward_copy(m).wait_recv()

        for i in range(share):
            for cc in range(2):
                if i + cc > 0:
                    @pl.when((stage == 0) & (core == cc) & (m == i * micro_part))
                    def _():
                        extra_copy(0, 0, i).wait_recv()

        for k in range(per):
            @pl.when((stage == 0) & (m == 0))
            def _():
                weights_here(k)

            x = left[0, k, at, :]
            pre = jnp.dot(x, full[0, k], preferred_element_type=jnp.float32)
            sig = jax.nn.sigmoid(pre)
            h = (pre * sig).astype(jnp.bfloat16)
            left[1, k, at, :] = h
            ds[k, at, :] = sig * (1.0 + pre * (1.0 - sig))
            y = (
                x.astype(jnp.float32)
                + jnp.dot(h, full[1, k], preferred_element_type=jnp.float32)
            ).astype(jnp.bfloat16)
            if k + 1 < per:
                left[0, k + 1, at, :] = y
            else:
                ysend[at, :] = y

        @pl.when(stage < stages - 1)
        def _():
            forward_copy(m).start()

        return carry

    def transpose_weights():
        for mat in range(2):
            for k in range(per):
                full_t[mat, k] = full[mat, k].T

    @pl.when(stage >= stages // 2)
    def _():
        transpose_weights()

    lax.fori_loop(0, micro, forward, 0)

    @pl.when(stage < stages // 2)
    def _():
        transpose_weights()

    def backward(m, carry):
        at = block(m, tile)

        @pl.when(stage < stages - 1)
        def _():
            backward_copy(m).wait_recv()

        for i in range(share):
            for cc in range(2):
                if cc * share + i != b_end:
                    @pl.when((stage == stages - 1) & (core == cc) & (m == i * micro_part))
                    def _():
                        extra_copy(1, b_end, i).wait_recv()

        for k in reversed(range(per)):
            dy = right[1, k, at, :]
            dh = jnp.dot(dy, full_t[1, k], preferred_element_type=jnp.float32)
            dp = (dh * ds[k, at, :]).astype(jnp.bfloat16)
            right[0, k, at, :] = dp
            dx = (
                dy.astype(jnp.float32)
                + jnp.dot(dp, full_t[0, k], preferred_element_type=jnp.float32)
            ).astype(jnp.bfloat16)
            if k > 0:
                right[1, k - 1, at, :] = dx
            else:
                dxsend[at, :] = dx

        @pl.when(stage > 0)
        def _():
            backward_copy(m).start()

        return carry

    lax.fori_loop(0, micro, backward, 0)

    def swap_copy(k):
        return pltpu.make_async_remote_copy(
            src_ref=gsend.at[k],
            dst_ref=gpeer.at[k],
            send_sem=x_tx.at[k],
            recv_sem=x_rx.at[k],
            device_id=(mate, d),
            device_id_type=MESH,
        )

    def grad_copy(k, t, slot):
        e = half * per + k
        return pltpu.make_async_remote_copy(
            src_ref=gtotal.at[k, block(t, wr)],
            dst_ref=grecv.at[core, rep, lax.rem(e, layers)],
            send_sem=g_tx.at[k, slot],
            recv_sem=g_rx.at[core, rep, lax.rem(e, layers)],
            device_id=(2 * col + e // layers, t),
            device_id_type=MESH,
        )

    def product(mat, k):
        for c in range(share):
            at = pl.ds(c * part, part)
            term = lax.dot_general(
                left[mat, k, at, :], right[mat, k, at, :], TN, preferred_element_type=jnp.float32
            )
            acc[...] = term if c == 0 else acc[...] + term

    for k in reversed(range(per)):
        e = half * per + k
        product(1 - core, k)
        gsend[k] = acc[...].astype(jnp.bfloat16)
        swap_copy(k).start()
        product(core, k)
        swap_copy(k).wait_recv()
        gtotal[k] = (acc[...] + gpeer[k].astype(jnp.float32)).astype(jnp.bfloat16)
        for o in sorted(range(1, n_d), key=lambda o: -min(o, n_d - o)):
            grad_copy(k, lax.rem(d + o, n_d), o).start()

        @pl.when(e // layers != core)
        def _():
            grad_copy(k, d, 0).start()

        @pl.when(e // layers == core)
        def _():
            grecv[core, rep, lax.rem(e, layers)] = gtotal[k, block(d, wr), :]

    for layer in reversed(range(layers)):
        for mat in (1, 0):
            for r in range(reps):
                t = host(r, (core * layers + layer) // per)

                @pl.when((t != d) | (core != mat))
                def _():
                    pltpu.make_async_remote_copy(
                        src_ref=gtotal.at[0, pl.ds(0, wr)],
                        dst_ref=grecv.at[mat, r, layer],
                        send_sem=g_tx.at[0, 0],
                        recv_sem=g_rx.at[mat, r, layer],
                        device_id=(mate, d),
                        device_id_type=MESH,
                    ).wait_recv()

            total = grecv[mat, 0, layer].astype(jnp.float32)
            for r in range(1, reps):
                total += grecv[mat, r, layer].astype(jnp.float32)
            w, out = ((w_in, new_in), (w_out, new_out))[mat]
            out[0, layer] = w[0, layer].astype(jnp.float32) - rate * total

    for layer in range(layers):
        for mat in range(2):
            for r in range(reps):
                weight_copy(mat, layer, r).wait_send()
    for k in range(per):
        e = half * per + k
        swap_copy(k).wait_send()
        for o in range(1, n_d):
            pass_copy(core, k, lax.rem(d + o, n_d), o - 1).wait_send()
            grad_copy(k, lax.rem(d + o, n_d), o).wait_send()

        @pl.when(e // layers != core)
        def _():
            grad_copy(k, d, 0).wait_send()

    @pl.when(feed_in)
    def _():
        extra_copy(0, 0, slot_of).wait_send()

    @pl.when(feed_out)
    def _():
        extra_copy(1, b_end, slot_of).wait_send()

    def drain(m, carry):
        @pl.when(stage < stages - 1)
        def _():
            forward_copy(m).wait_send()

        @pl.when(stage > 0)
        def _():
            backward_copy(m).wait_send()

        return carry

    lax.fori_loop(0, micro, drain, 0)


def solution(mesh):
    n_s, n_d = mesh.shape["section"], mesh.shape["dp"]

    def per_device(images, cotangent, w_in, w_out):
        micro, pixels, width = images.shape
        layers, wr = w_in.shape[1:3]
        part = micro * pixels
        group, tile = GROUP, ROWS
        rows, per, reps = group // 2 * part, 2 * layers // group, n_d // group
        steps = rows // tile
        bf, f32 = jnp.bfloat16, jnp.float32
        rate = 0.1 / math.sqrt(part * n_d)
        dma = pltpu.SemaphoreType.DMA
        vmem = pl.BlockSpec(memory_space=pltpu.VMEM)
        return pl.pallas_call(
            functools.partial(kernel, n_s, n_d, group, tile, rate),
            out_shape=(
                jax.ShapeDtypeStruct(w_in.shape, f32),
                jax.ShapeDtypeStruct(w_out.shape, f32),
            ),
            in_specs=[vmem] * 4,
            out_specs=(vmem, vmem),
            scratch_shapes=[
                pltpu.VMEM((2, per, rows, width), bf),
                pltpu.VMEM((2, per, rows, width), bf),
                pltpu.VMEM((per, rows, width), f32),
                pltpu.VMEM((rows, width), bf),
                pltpu.VMEM((rows, width), bf),
                pltpu.VMEM((2, per, width, width), bf),
                pltpu.VMEM((2, per, width, width), bf),
                pltpu.VMEM((width, width), f32),
                pltpu.VMEM((per, width, width), bf),
                pltpu.VMEM((per, width, width), bf),
                pltpu.VMEM((per, width, width), bf),
                pltpu.VMEM((2, reps, layers, wr, width), bf),
                dma((steps,)), dma((steps,)), dma((steps,)), dma((steps,)),
                dma((2, layers, reps)), dma((2, per, n_d)), dma((per, n_d - 1)),
                dma((per, n_d)), dma((2, reps, layers)),
                dma((per,)), dma((per,)),
                dma((2,)), dma((2, group // 2)),
            ],
            compiler_params=pltpu.CompilerParams(
                collective_id=0, has_side_effects=True, vmem_limit_bytes=56 * 1024 * 1024
            ),
            cost_estimate=pl.CostEstimate(
                flops=12 * part * layers * width * width, bytes_accessed=8 << 20, transcendentals=0
            ),
        )(images.reshape(part, width), cotangent.reshape(part, width), w_in, w_out)

    in_specs = (
        P(None, "dp", None),
        P(None, "dp", None),
        P("section", None, "dp", None),
        P("section", None, "dp", None),
    )
    out_specs = (P("section", None, "dp", None), P("section", None, "dp", None))
    return jax.shard_map(
        per_device, mesh=mesh, in_specs=in_specs, out_specs=out_specs, check_vma=False
    )
```
